512 devices in a mesh: tok: 8 (over x, core), exp: 64 (over y, z).
Axes of the slice: x: 4, y: 8, z: 8, core: 2. Of those that a mesh axis runs over, the one named last changes fastest.
Arguments:
- tokens: bfloat16 [4096, 16384], P('exp', 'tok'), as said below
- w_router: bfloat16 [4096, 256], P('exp'), as said below
- pick_lists: int32 [8, 64, 16], P('tok'), may hold values from 0 to 2047, as said below
- w_gate: bfloat16 [64, 4096, 1024], P('exp', None, 'tok'), may hold values from -0.09375 to 0.09375
- w_up: bfloat16 [64, 4096, 1024], P('exp', None, 'tok'), may hold values from -0.09375 to 0.09375
- w_down: bfloat16 [64, 1024, 4096], P('exp', 'tok'), may hold values from -0.1875 to 0.1875
- out_grad: bfloat16 [4096, 16384], P('exp', 'tok'), may hold values from -6 to 6
Outputs:
- layer_out: bfloat16 [4096, 16384], P('exp', 'tok')
- token_grad: bfloat16 [4096, 16384], P('exp', 'tok')
- grad_router: float32 [4096, 256], P('exp')
The draws below stay inside these ranges and needn't reach their ends.
Inputs may be any that keep to these rules, and one draw needn't show every extreme that they name: `pick_lists`: each of the 64 lists of a group names 16 distinct positions among the group's 2048 tokens. `tokens`: activations. `w_router`: router weights.
All inputs are finite; a program needn't handle non-finite values.
Results may differ from the reference program's by a relative error of at most 0.024.
Values may be sent and summed in bfloat16 or wider, within the bound.
A program may use at most 64 MiB of HBM per device.

```python
import math
import jax
import jax.numpy as jnp
from jax import lax

D = 4096
FF = 1024
EXP_COLS = 4
GROUP = 2048
EXPERTS = 256
CAP = 16
ROWS = 128
TOKENS = 16384
N_TOK = 8
N_EXP = 64


def token_field(key):
    base_key, scale_key = jax.random.split(key)
    base = jnp.clip(jax.random.normal(base_key, (D, TOKENS), jnp.float32), -5.0, 5.0)
    scales = jnp.exp(jax.random.uniform(scale_key, (1, TOKENS), jnp.float32, math.log(0.5), math.log(2.0)))
    return base * scales


def draw_tokens(key, part):
    return token_field(key).astype(jnp.bfloat16)


def draw_w_router(key, part):
    key = jax.random.fold_in(key, 7)
    normal_key, scale_key, sign_key = jax.random.split(key, 3)
    ramp = 3.0 ** (jnp.arange(EXPERTS, dtype=jnp.float32) / (EXPERTS - 1))
    spread = jnp.exp(jax.random.uniform(scale_key, (EXPERTS,), jnp.float32, math.log(0.5), math.log(1.5)))
    weights = jax.random.normal(normal_key, (D, EXPERTS), jnp.float32) * (0.3 * ramp * spread)[None, :] / math.sqrt(D)
    common_sign = jnp.where(jax.random.bernoulli(sign_key, 0.5, (D,)), 1.0, -1.0).astype(jnp.float32)
    return (weights + 120.0 / math.sqrt(D) * common_sign[:, None]).astype(jnp.bfloat16)


def draw_pick_lists(key, part):
    key = jax.random.fold_in(key, 11)
    main_key, edge_key = jax.random.split(key)
    list_keys = jax.random.split(main_key, N_TOK * N_EXP)
    lists = jax.vmap(lambda one_key: jax.random.permutation(one_key, GROUP)[:CAP])(list_keys)
    lists = lists.reshape(N_TOK, N_EXP, CAP).astype(jnp.int32)
    inner = jnp.arange(1, GROUP - 1, dtype=jnp.int32)

    def edge_list(one_key):
        first_key, order_key = jax.random.split(one_key)
        chosen = jnp.concatenate((jnp.array([0, GROUP - 1], jnp.int32), jax.random.permutation(first_key, inner)[:CAP - 2]))
        return jax.random.permutation(order_key, chosen)
    edges = jax.vmap(edge_list)(jax.random.split(edge_key, N_TOK)).astype(jnp.int32)
    return lists.at[:, 0, :].set(edges)


def steps_of(key, extent, pieces, low, top_value):
    loudness = 1.0
    for axis_at, blocks in pieces:
        heights = jax.random.uniform(jax.random.fold_in(jax.random.fold_in(key, 6), axis_at), (blocks,), jnp.float32, low / len(pieces), top_value / len(pieces))
        loudness = loudness * jnp.repeat(jnp.exp(heights), extent[axis_at] // blocks).reshape((-1,) + (1,) * (len(extent) - 1 - axis_at))
    return loudness


def noise(stream_key, shape, deviation, reach, cuts=(), held_as=jnp.bfloat16):
    values = jax.random.normal(stream_key, shape, jnp.float32) * deviation
    if len(cuts) > 0:
        values = steps_of(stream_key, shape, cuts, -0.22, 0.18) * values
    return jnp.clip(values, min=-reach, max=reach).astype(held_as)


def setup_inputs(seed: int = 0) -> dict:
    key_of = jax.random.split(jax.random.key(seed), 8)
    tokens = draw_tokens(jax.random.fold_in(key_of[7], 71), 0)
    w_router = draw_w_router(jax.random.fold_in(key_of[7], 71), 0)
    pick_lists = draw_pick_lists(jax.random.fold_in(key_of[7], 71), 0)
    w_gate = noise(key_of[3], (N_EXP, D, FF), D ** -0.5, 0.09375, ((0, 64), (2, 8)))
    w_up = noise(key_of[4], (N_EXP, D, FF), D ** -0.5, 0.09375, ((0, 64), (2, 8)))
    w_down = noise(key_of[5], (N_EXP, FF, D), FF ** -0.5, 0.1875, ((0, 64), (1, 8)))
    out_grad = noise(key_of[6], (D, TOKENS), 1.0, 6.0, ((0, 64), (1, 8)))
    return {"tokens": tokens, "w_router": w_router, "pick_lists": pick_lists, "w_gate": w_gate, "w_up": w_up, "w_down": w_down, "out_grad": out_grad}


def expert_pass(tokens, out_grad, pick_order, pick_weight, gate_weight, up_weight, down_weight):
    block = FF // N_TOK
    token_rows = tokens[:, pick_order].T
    grad_rows = out_grad[:, pick_order].T.astype(jnp.float32)
    pre_gate = jnp.dot(token_rows, gate_weight, preferred_element_type=jnp.float32)
    pre_up = jnp.dot(token_rows, up_weight, preferred_element_type=jnp.float32)
    hidden = (jax.nn.silu(pre_gate) * pre_up).astype(jnp.bfloat16)
    partial_out = jnp.einsum("rnf,nfd->nrd", hidden.reshape(ROWS, N_TOK, block).astype(jnp.float32),
                             down_weight.reshape(N_TOK, block, D).astype(jnp.float32))
    rounded_out = lax.optimization_barrier(partial_out.astype(jnp.bfloat16))
    expert_out = jnp.sum(rounded_out.astype(jnp.float32), axis=0)
    weighted = (pick_weight[:, None] * expert_out).astype(jnp.bfloat16)
    gate_grad = jnp.sum(grad_rows * expert_out, axis=1)
    row_grad = (pick_weight[:, None] * grad_rows).astype(jnp.bfloat16)
    hidden_grad = jnp.dot(row_grad, down_weight.T, preferred_element_type=jnp.float32)
    sigmoid_gate = jax.nn.sigmoid(pre_gate)
    grad_gate_pre = (hidden_grad * pre_up * sigmoid_gate * (1.0 + pre_gate * (1.0 - sigmoid_gate))).astype(jnp.bfloat16)
    grad_up_pre = (hidden_grad * pre_gate * sigmoid_gate).astype(jnp.bfloat16)
    partial_in = jnp.einsum("rnf,dnf->nrd", grad_gate_pre.reshape(ROWS, N_TOK, block).astype(jnp.float32),
                            gate_weight.reshape(D, N_TOK, block).astype(jnp.float32))
    partial_in = partial_in + jnp.einsum("rnf,dnf->nrd", grad_up_pre.reshape(ROWS, N_TOK, block).astype(jnp.float32),
                                         up_weight.reshape(D, N_TOK, block).astype(jnp.float32))
    rounded_in = lax.optimization_barrier(partial_in.astype(jnp.bfloat16))
    row_input = jnp.sum(rounded_in.astype(jnp.float32), axis=0).astype(jnp.bfloat16)
    return weighted, row_input, gate_grad


def reference(tokens, w_router, pick_lists, w_gate, w_up, w_down, out_grad):
    logits = jnp.dot(w_router.T, tokens, preferred_element_type=jnp.float32)
    peak_score = jnp.max(logits, axis=0, keepdims=True)
    expo_score = jnp.exp(logits - peak_score)
    router_probs = expo_score / jnp.sum(expo_score, axis=0, keepdims=True)
    offsets = (jnp.arange(N_TOK, dtype=jnp.int32) * GROUP)[:, None, None]
    pick_order = jnp.transpose(pick_lists + offsets, (1, 0, 2)).reshape(N_EXP, ROWS)
    columns = jnp.arange(N_EXP, dtype=jnp.int32) * EXP_COLS
    flight_probs = router_probs[columns]
    pick_weight = jnp.take_along_axis(flight_probs, pick_order, axis=1)

    def one_expert(inputs):
        return expert_pass(tokens, out_grad, inputs[0], inputs[1], inputs[2], inputs[3], inputs[4])

    weighted, row_input, gate_grad = lax.map(one_expert, (pick_order, pick_weight, w_gate, w_up, w_down))
    flat_order = pick_order.reshape(-1)
    layer_out = jnp.zeros((D, TOKENS), jnp.float32).at[:, flat_order].add(
        weighted.reshape(N_EXP * ROWS, D).T.astype(jnp.float32))
    score_grad = jnp.zeros((EXPERTS, TOKENS), jnp.float32).at[columns[:, None], pick_order].add(gate_grad)
    pick_sum = jnp.sum(router_probs * score_grad, axis=0, keepdims=True)
    logit_grad = router_probs * (score_grad - pick_sum)
    router_part = jnp.dot(w_router.astype(jnp.float32), logit_grad, precision=lax.Precision.HIGHEST)
    row_part = jnp.zeros((D, TOKENS), jnp.float32).at[:, flat_order].add(
        row_input.reshape(N_EXP * ROWS, D).T.astype(jnp.float32))
    token_grad = (router_part + row_part).astype(jnp.bfloat16)
    grad_router = jnp.dot(tokens.astype(jnp.float32), logit_grad.T, precision=lax.Precision.HIGHEST)
    return layer_out.astype(jnp.bfloat16), token_grad, grad_router
```

```python
import jax
import jax.numpy as jnp
from jax import lax
from jax.experimental import pallas as pl
from jax.experimental.pallas import tpu as pltpu
from jax.sharding import PartitionSpec as P

MESH = pl.DeviceIdType.MESH
BF = jnp.bfloat16
F32 = jnp.float32
NE = 64
NT = 8
CAP = 16
COLS = 4
NEAR = (0, 1, 7, 2, 6, 3, 5, 4)
FAR = (4, 3, 5, 2, 6, 1, 7, 0)
NN = (((1,), (0,)), ((), ()))
NTD = (((1,), (1,)), ((), ()))
TND = (((0,), (0,)), ((), ()))


def dot(a, b, dims):
    return lax.dot_general(a, b, dims, preferred_element_type=F32)


def remote(src, dst, send, recv, **where):
    return pltpu.make_async_remote_copy(
        src, dst, send, recv, device_id=where, device_id_type=MESH
    )


def kernel(
    tk, og, wr, plb, wg_h, wu_h, wd_h,
    out_layer, out_token, out_router,
    PT, S, R, G2, WS, WM, WRF, WG, WU, WD, ACC, ACT,
    PB, SB, PS, B1, B2, B3, C2, GPB, GPR, LQ, LQM, LQR, TS, TR, GRP, GRR, GRO, GRF, D3,
    wsem, loc, d_s, d_r, g_s, g_r, w1_s, w1_r, w2_s, w2_r, w3_s, w3_r,
    r_s, r_r, gg_s, gg_r, l1_s, l1_r, l2_s, l2_r, t_s, t_r, q1_s, q1_r, q2_s, q2_r,
):
    t = lax.axis_index("tok")
    me = lax.axis_index("exp")
    core = lax.rem(t, 2)
    x = t // 2
    y = me // 8
    z = lax.rem(me, 8)
    xr, xl, xo = lax.rem(x + 1, 4), lax.rem(x + 3, 4), lax.rem(x + 2, 4)
    sib = t + 1 - 2 * core
    right, left, opp = 2 * xr + core, 2 * xl + core, 2 * xo + core
    a = jnp.where(core == 0, y, z)
    b = jnp.where(core == 0, z, y)
    sa = jnp.where(core == 0, 8, 1)
    sb = jnp.where(core == 0, 1, 8)

    barrier = pltpu.get_barrier_semaphore()

    @pl.loop(1, NE)
    def _(k):
        pl.semaphore_signal(
            barrier, inc=1, device_id={"exp": lax.rem(me + k, NE)}, device_id_type=MESH
        )

    @pl.loop(1, NT)
    def _(k):
        pl.semaphore_signal(
            barrier, inc=1, device_id={"tok": lax.rem(t + k, NT)}, device_id_type=MESH
        )

    local = [
        pltpu.make_async_copy(wg_h, WG, wsem.at[0]),
        pltpu.make_async_copy(wu_h, WU, wsem.at[1]),
    ]
    for i in range(8):
        local.append(
            pltpu.make_async_copy(wd_h.at[:, pl.ds(512 * i, 512)], WD.at[i], wsem.at[2 + i])
        )
    for c in local:
        c.start()

    WS[...] = jnp.where(core == 0, wr[:, :128], wr[:, 128:])
    lane = lax.broadcasted_iota(jnp.int32, (128, 128), 1)

    @pl.loop(0, 8)
    def _(i):
        rows = pl.ds(pl.multiple_of(i * 128, 128), 128)
        pos = plb[rows, :]
        for c in range(16):
            PT[rows, c * 128 : (c + 1) * 128] = jnp.where(pos == lane + 128 * c, 1.0, 0.0).astype(BF)
        oh = PT[rows, :]
        got = jnp.concatenate((dot(oh, tk[...], NTD), dot(oh, og[...], NTD)), axis=1)
        S[pl.ds(i * 8, 8)] = got.astype(BF).reshape(8, 16, 128)

    pl.semaphore_wait(barrier, NE - 1 + NT - 1)

    for i, sh in enumerate(NEAR):
        row = lax.rem(y + sh, 8)

        @pl.loop(1 if sh == 0 else 0, 8)
        def _(k):
            d = row * 8 + lax.rem(z + k, 8)
            remote(S.at[d], R.at[me], d_s, d_r.at[i], exp=d).start()

        if sh == 0:
            pltpu.make_async_copy(S.at[me], R.at[me], d_r.at[0]).start()

    own_half = pltpu.make_async_copy(WS, WM.at[a], loc.at[0])
    own_half.start()
    w1 = []
    for k in range(1, 8):
        w1.append(remote(WS, WM.at[a], w1_s, w1_r, exp=lax.rem(a + k, 8) * sa + b * sb))
        w1[-1].start()

    def router_second():
        own_half.wait()
        seven = WM.at[pl.ds(0, 7)]
        remote(seven, seven, w1_s, w1_r, exp=me).wait_recv()
        cs = []
        for k in range(1, 8):
            cs.append(
                remote(WM, WRF.at[core, b], w2_s, w2_r.at[k], exp=a * sa + lax.rem(b + k, 8) * sb)
            )
            cs[-1].start()
        c = pltpu.make_async_copy(WM, WRF.at[core, b], loc.at[1])
        c.start()
        c.wait()
        cs.append(remote(WRF.at[core, b], WRF.at[core, b], w3_s.at[0], w3_r.at[0], tok=sib))
        cs[-1].start()
        return cs

    def router_third(k):
        src = lax.rem(b + 8 - k, 8)
        remote(WM, WRF.at[core, src], w2_s, w2_r.at[k], exp=me).wait_recv()
        c = remote(WRF.at[core, src], WRF.at[core, src], w3_s.at[k], w3_r.at[k], tok=sib)
        c.start()
        return c

    low = lax.broadcasted_iota(jnp.int32, (16, 128), 1) < 64
    sent = []
    kept = {}

    def go(key, c):
        c.start()
        sent.append(c)
        kept[key] = c

    def gather_own(i):
        row = lax.rem(y + 8 - NEAR[i], 8)
        eight = R.at[pl.ds(row * 8, 8)]
        remote(eight, eight, d_s, d_r.at[i], exp=me).wait_recv()
        for m in range(4):
            p = R[row * 8 + 2 * m].astype(F32)
            q = R[row * 8 + 2 * m + 1].astype(F32)
            cols = slice(128 * m, 128 * m + 128)
            G2[row, t, 0, :, cols] = jnp.where(low, p, pltpu.roll(q, 64, 1)).astype(BF)
            G2[row, t, 1, :, cols] = jnp.where(low, pltpu.roll(p, 64, 1), q).astype(BF)
        blk = G2.at[row, t]
        go((0, i), remote(blk, blk, g_s.at[0, i], g_r.at[0, i], tok=right))
        go((1, i), remote(blk, blk, g_s.at[1, i], g_r.at[1, i], tok=left))
        go((2, i), remote(blk, blk, g_s.at[2, i], g_r.at[2, i], tok=sib))

    def gather_next(i):
        row = lax.rem(y + 8 - NEAR[i], 8)
        blk = G2.at[row, left]
        remote(blk, blk, g_s.at[0, i], g_r.at[0, i], tok=right).wait_recv()
        part = G2.at[row, left, 0]
        go((3, i), remote(part, part, g_s.at[3, i], g_r.at[3, i], tok=right))
        go((4, i), remote(blk, blk, g_s.at[4, i], g_r.at[4, i], tok=sib))
        blk = G2.at[row, right]
        remote(blk, blk, g_s.at[1, i], g_r.at[1, i], tok=left).wait_recv()
        part = G2.at[row, right, 1]
        go((5, i), remote(part, part, g_s.at[5, i], g_r.at[5, i], tok=left))
        go((6, i), remote(blk, blk, g_s.at[6, i], g_r.at[6, i], tok=sib))

    def gather_far(i):
        row = lax.rem(y + 8 - NEAR[i], 8)
        for h, kind in ((0, 3), (1, 5)):
            part = G2.at[row, opp, h]
            remote(part, part, g_s.at[kind, i], g_r.at[kind, i], tok=right).wait_recv()
            go((7 + h, i), remote(part, part, g_s.at[7 + h, i], g_r.at[7 + h, i], tok=sib))

    def gather_done(i):
        row = lax.rem(y + 8 - NEAR[i], 8)
        side = 1 - core
        for kind, who in ((2, sib), (4, 2 * xl + side), (6, 2 * xr + side)):
            blk = G2.at[row, who]
            remote(blk, blk, g_s.at[kind, i], g_r.at[kind, i], tok=sib).wait_recv()
        for h in (0, 1):
            part = G2.at[row, 2 * xo + side, h]
            remote(part, part, g_s.at[7 + h, i], g_r.at[7 + h, i], tok=sib).wait_recv()
        rows = G2[row, :, 0].reshape(128, 512)
        grads = G2[row, :, 1].reshape(128, 512)
        k = pl.ds(pl.multiple_of(row * 512, 512), 512)
        parts = (dot(rows, WG[k, :], NN), dot(rows, WU[k, :], NN), dot(grads, WD[row], NTD))
        for n, part in enumerate(parts):
            ACC[n] = part if i == 0 else ACC[n] + part

    w2 = None
    w3 = []
    for s in range(11):
        if s < 8:
            gather_own(s)
        if s == 4:
            w2 = router_second()
        if 1 <= s < 9:
            gather_next(s - 1)
        if 2 <= s < 10:
            gather_far(s - 2)
        if s == 3:
            for c in local:
                c.wait()
        if 3 <= s:
            gather_done(s - 3)

    pre_gate, pre_up, back = ACC[0], ACC[1], ACC[2]
    sg = jax.nn.sigmoid(pre_gate)
    hidden = (pre_gate * sg * pre_up).astype(BF)
    ACT[0] = hidden
    ACT[1] = (back * pre_up * sg * (1.0 + pre_gate * (1.0 - sg))).astype(BF)
    ACT[2] = (back * pre_gate * sg).astype(BF)
    gsum = jnp.sum(hidden.astype(F32) * back, axis=1, keepdims=True)
    GPB[...] = jnp.broadcast_to(gsum, (128, 128)).reshape(8, 16, 128)
    for k in range(1, 8):
        d = lax.rem(t + k, 8)
        remote(GPB.at[d], GPR.at[t], gg_s, gg_r, tok=d).start()
    pltpu.make_async_copy(GPB.at[t], GPR.at[t], gg_r).start()

    def sum_make(i):
        row = lax.rem(y + FAR[i], 8)
        k = pl.ds(pl.multiple_of(row * 512, 512), 512)
        eo = dot(ACT[0], WD[row], NN)
        PB[i, 0] = eo.astype(BF).reshape(4, 2, 16, 512)
        ri = dot(ACT[1], WG[k, :], NTD) + dot(ACT[2], WU[k, :], NTD)
        PB[i, 1] = ri.astype(BF).reshape(4, 2, 16, 512)
        go(("sib", i), remote(PB.at[i, :, :, 1 - core], SB.at[i], r_s.at[0, i], r_r.at[0, i], tok=sib))

    def sum_pair(i):
        kept["sib", i].wait_recv()
        PS[i] = (PB[i, :, :, core].astype(F32) + SB[i].astype(F32)).astype(BF)
        go(("le", i), remote(PS.at[i, 0, xo], B1.at[i, 0], r_s.at[1, i], r_r.at[1, i], tok=right))
        go(("lr", i), remote(PS.at[i, 1, xo], B1.at[i, 1], r_s.at[2, i], r_r.at[2, i], tok=left))
        go(("de", i), remote(PS.at[i, 0, xl], B3.at[i, 0], r_s.at[3, i], r_r.at[3, i], tok=left))
        go(("dr", i), remote(PS.at[i, 1, xr], B3.at[i, 1], r_s.at[4, i], r_r.at[4, i], tok=right))

    def sum_next(i):
        kept["le", i].wait_recv()
        C2[i, 0] = (PS[i, 0, xr].astype(F32) + B1[i, 0].astype(F32)).astype(BF)
        go(("ce", i), remote(C2.at[i, 0], B2.at[i, 0], r_s.at[5, i], r_r.at[5, i], tok=right))
        kept["lr", i].wait_recv()
        C2[i, 1] = (PS[i, 1, xl].astype(F32) + B1[i, 1].astype(F32)).astype(BF)
        go(("cr", i), remote(C2.at[i, 1], B2.at[i, 1], r_s.at[6, i], r_r.at[6, i], tok=left))

    def router():
        logits = [jnp.zeros((16, 128), F32), jnp.zeros((16, 128), F32)]
        for r in range(8):
            own = G2[r, t, 0]
            logits[0] += dot(own, WRF[0, :, r].reshape(512, 128), NN)
            logits[1] += dot(own, WRF[1, r].reshape(512, 128), NN)
        peak = jnp.maximum(
            jnp.max(logits[0], axis=1, keepdims=True), jnp.max(logits[1], axis=1, keepdims=True)
        )
        ex = [jnp.exp(v - peak) for v in logits]
        total = jnp.sum(ex[0], axis=1, keepdims=True) + jnp.sum(ex[1], axis=1, keepdims=True)
        probs = [v / total for v in ex]
        at = lax.broadcasted_iota(jnp.int32, (16, 128), 1)
        hit = [at == me * COLS, at + 128 == me * COLS]
        weight = sum(
            jnp.sum(jnp.where(m, v, 0.0), axis=1, keepdims=True) for m, v in zip(hit, probs)
        )
        eight = GPR.at[pl.ds(0, 8)]
        remote(eight, eight, gg_s, gg_r, tok=t).wait_recv()
        gate = GPR[0]
        for k in range(1, 8):
            gate = gate + GPR[k]
        scale = gate * weight
        for n in range(2):
            diff = jnp.where(hit[n], 1.0, 0.0) - probs[n]
            LQ[:, 128 * n : 128 * n + 128] = (diff * scale).astype(BF)
            for p in range(3):
                piece = diff.astype(BF)
                D3[n, 16 * p : 16 * p + 16] = piece
                diff = diff - piece.astype(F32)
        own_lq = pltpu.make_async_copy(LQ, LQM.at[a], loc.at[2])
        own_lq.start()
        for k in range(1, 8):
            remote(LQ, LQM.at[a], l1_s, l1_r, exp=lax.rem(a + k, 8) * sa + b * sb).start()
        return weight, scale, own_lq

    def router_grad_second(own_lq):
        own_lq.wait()
        seven = LQM.at[pl.ds(0, 7)]
        remote(seven, seven, l1_s, l1_r, exp=me).wait_recv()
        for k in range(1, 8):
            remote(LQM, LQR.at[b], l2_s, l2_r, exp=a * sa + lax.rem(b + k, 8) * sb).start()
        own = pltpu.make_async_copy(LQM, LQR.at[b], loc.at[3])
        own.start()
        return own

    def router_grad_sum(own):
        own.wait()
        seven = LQR.at[pl.ds(0, 7)]
        remote(seven, seven, l2_s, l2_r, exp=me).wait_recv()
        total = jnp.zeros((128, 256), F32)
        Sv = S[...].reshape(8, 8, 16, 128)
        for n in range(8):
            rows = jnp.where(core == 0, Sv[:, n].astype(F32), Sv[n].astype(F32)).astype(BF)
            total = total + dot(rows.reshape(128, 128), LQR[n].reshape(128, 256), TND)
        GRP[...] = total[:64].reshape(8, 8, 256)
        for k in range(1, 8):
            d = lax.rem(t + k, 8)
            remote(GRP.at[d], GRR.at[t], q1_s, q1_r, tok=d).start()
        pltpu.make_async_copy(GRP.at[t], GRR.at[t], q1_r).start()

    def router_grad_share():
        eight = GRR.at[pl.ds(0, 8)]
        remote(eight, eight, q1_s, q1_r, tok=t).wait_recv()
        total = GRR[0]
        for k in range(1, 8):
            total = total + GRR[k]
        GRO[...] = total
        for k in range(1, 8):
            remote(GRO, GRF.at[t], q2_s, q2_r, tok=lax.rem(t + k, 8)).start()
        pltpu.make_async_copy(GRO, GRF.at[t], q2_r).start()

    def finish(i, weight, scale):
        row = lax.rem(y + FAR[i], 8)
        for key in ("de", "dr", "ce", "cr"):
            kept[key, i].wait_recv()
        eo = PS[i, 0, x].astype(F32) + B2[i, 0].astype(F32) + B3[i, 0].astype(F32)
        ri = PS[i, 1, x].astype(F32) + B2[i, 1].astype(F32) + B3[i, 1].astype(F32)
        v3 = dot(D3[0], WRF[0, :, row].reshape(512, 128), NTD)
        v3 = v3 + dot(D3[1], WRF[1, row].reshape(512, 128), NTD)
        v = v3[0:16] + v3[16:32] + v3[32:48]
        for m in range(4):
            cols = slice(128 * m, 128 * m + 128)
            w = eo[:, cols] * weight
            g = ri[:, cols] * weight + v[:, cols] * scale
            TS[row * 8 + 2 * m] = jnp.where(low, w, pltpu.roll(g, 64, 1)).astype(BF)
            TS[row * 8 + 2 * m + 1] = jnp.where(low, pltpu.roll(w, 64, 1), g).astype(BF)

        @pl.loop(1 if FAR[i] == 0 else 0, 8)
        def _(k):
            d = row * 8 + lax.rem(z + k, 8)
            remote(TS.at[d], TR.at[me], t_s, t_r, exp=d).start()

        if FAR[i] == 0:
            pltpu.make_async_copy(TS.at[me], TR.at[me], t_r).start()

    for s in range(3):
        sum_make(s)
        if s >= 1:
            sum_pair(s - 1)
        if s >= 2:
            sum_next(s - 2)
    for k in range(1, 8):
        w3.append(router_third(k))
    for k in range(8):
        src = lax.rem(jnp.where(core == 0, y, z) + 8 - k, 8)
        blk = WRF.at[1 - core, src]
        remote(blk, blk, w3_s.at[k], w3_r.at[k], tok=sib).wait_recv()
    weight, scale, own_lq = router()
    own = None
    for s in range(3, 11):
        if s < 8:
            sum_make(s)
        if s < 9:
            sum_pair(s - 1)
        if s < 10:
            sum_next(s - 2)
        finish(s - 3, weight, scale)
        if s == 5:
            own = router_grad_second(own_lq)
    router_grad_sum(own)
    router_grad_share()

    every = TR.at[pl.ds(0, 64)]
    remote(every, every, t_s, t_r, exp=me).wait_recv()
    back_rows = TR[...].reshape(1024, 128)

    for c in range(4):
        cols = slice(512 * c, 512 * c + 512)
        res = dot(back_rows, PT[:, cols], TND)
        out_layer[:, cols] = res[:64].astype(BF)
        out_token[:, cols] = res[64:].astype(BF)

    eight = GRF.at[pl.ds(0, 8)]
    remote(eight, eight, q2_s, q2_r, tok=t).wait_recv()
    out_router[...] = GRF[...].reshape(64, 256)

    for c in sent + w3 + w2[7:]:
        c.wait_send()
    n63 = S.at[pl.ds(0, 63)]
    remote(n63, n63, d_s, d_r.at[0], exp=me).wait_send()
    remote(n63, n63, t_s, t_r, exp=me).wait_send()
    n7 = WM.at[pl.ds(0, 7)]
    remote(n7, n7, w1_s, w1_r, exp=me).wait_send()
    n7 = WRF.at[0, pl.ds(0, 7)]
    remote(n7, n7, w2_s, w2_r.at[1], exp=me).wait_send()
    n7 = GPB.at[pl.ds(0, 7)]
    remote(n7, n7, gg_s, gg_r, tok=t).wait_send()
    n7 = LQM.at[pl.ds(0, 7)]
    remote(n7, n7, l1_s, l1_r, exp=me).wait_send()
    n7 = LQR.at[pl.ds(0, 7)]
    remote(n7, n7, l2_s, l2_r, exp=me).wait_send()
    n7 = GRP.at[pl.ds(0, 7)]
    remote(n7, n7, q1_s, q1_r, tok=t).wait_send()
    remote(n7, n7, q2_s, q2_r, tok=t).wait_send()


def body(tokens, w_router, pick_lists, w_gate, w_up, w_down, out_grad):
    flat = jnp.broadcast_to(pick_lists.reshape(NE * CAP, 1), (NE * CAP, 128))
    V = pltpu.VMEM
    D = pltpu.SemaphoreType.DMA
    vm = pl.BlockSpec(memory_space=pltpu.VMEM)
    hbm = pl.BlockSpec(memory_space=pl.ANY)
    scratch = [
        V((1024, 2048), BF),
        V((64, 16, 128), BF),
        V((64, 16, 128), BF),
        V((8, 8, 2, 16, 512), BF),
        V((64, 128), BF),
        V((8, 64, 128), BF),
        V((2, 8, 8, 64, 128), BF),
        V((4096, 128), BF),
        V((4096, 128), BF),
        V((8, 128, 512), BF),
        V((3, 128, 128), F32),
        V((3, 128, 128), BF),
        V((8, 2, 4, 2, 16, 512), BF),
        V((8, 2, 4, 16, 512), BF),
        V((8, 2, 4, 16, 512), BF),
        V((8, 2, 16, 512), BF),
        V((8, 2, 16, 512), BF),
        V((8, 2, 16, 512), BF),
        V((8, 2, 16, 512), BF),
        V((8, 16, 128), F32),
        V((8, 16, 128), F32),
        V((16, 256), BF),
        V((8, 16, 256), BF),
        V((8, 8, 16, 256), BF),
        V((64, 16, 128), BF),
        V((64, 16, 128), BF),
        V((8, 8, 256), F32),
        V((8, 8, 256), F32),
        V((8, 256), F32),
        V((8, 8, 256), F32),
        V((2, 48, 128), BF),
        D((10,)), D((4,)),
        D, D((8,)),
        D((9, 8)), D((9, 8)),
        D, D,
        D, D((8,)),
        D((8,)), D((8,)),
        D((7, 8)), D((7, 8)),
        D, D,
        D, D, D, D,
        D, D,
        D, D, D, D,
    ]
    return pl.pallas_call(
        kernel,
        out_shape=(
            jax.ShapeDtypeStruct((64, 2048), BF),
            jax.ShapeDtypeStruct((64, 2048), BF),
            jax.ShapeDtypeStruct((64, 256), F32),
        ),
        in_specs=[vm, vm, vm, vm, hbm, hbm, hbm],
        out_specs=(vm, vm, vm),
        scratch_shapes=scratch,
        compiler_params=pltpu.CompilerParams(
            collective_id=0, has_side_effects=True, vmem_limit_bytes=48 << 20
        ),
        cost_estimate=pl.CostEstimate(
            flops=3_000_000_000, bytes_accessed=8_000_000, transcendentals=40_000
        ),
        name="experts",
    )(tokens, out_grad, w_router, flat, w_gate[0], w_up[0], w_down[0])


def solution(mesh):
    placed = (
        P("exp", "tok"),
        P("exp", None),
        P("tok", None, None),
        P("exp", None, "tok"),
        P("exp", None, "tok"),
        P("exp", "tok", None),
        P("exp", "tok"),
    )
    return jax.shard_map(
        body,
        mesh=mesh,
        in_specs=placed,
        out_specs=(P("exp", "tok"), P("exp", "tok"), P("exp", None)),
        check_vma=False,
    )
```

```python
import jax
import jax.numpy as jnp
from jax import lax
from jax.experimental import pallas as pl
from jax.experimental.pallas import tpu as pltpu
from jax.sharding import PartitionSpec as P

MESH = pl.DeviceIdType.MESH
BF = jnp.bfloat16
F32 = jnp.float32
NE = 64
NT = 8
CAP = 16
COLS = 4
NEAR = (0, 1, 7, 2, 6, 3, 5, 4)
FAR = (4, 3, 5, 2, 6, 1, 7, 0)
AHEAD = 8
LAG = (3, 6, 8)
SLAG = (2, 4, 6)
RELAY = 8
ROUTE = (3, 6, 10, 13)
BACK = 3
NN = (((1,), (0,)), ((), ()))
NTD = (((1,), (1,)), ((), ()))
TND = (((0,), (0,)), ((), ()))


def dot(a, b, dims):
    return lax.dot_general(a, b, dims, preferred_element_type=F32)


def remote(src, dst, send, recv, **where):
    return pltpu.make_async_remote_copy(
        src, dst, send, recv, device_id=where, device_id_type=MESH
    )


def kernel(
    tk_h, og_h, wr_h, pl_h, wg_h, wu_h, wd_h,
    out_layer, out_token, out_router,
    TK, OG, WRL, PLV, PT, S, R, G2, WS, WM, WRF, WG, WU, WD, ACC, ACT,
    PB, SB, PS, B1, B2, B3, C2, GPB, GPR, LQ, LQM, LQR, TS, TR, GRP, GRR, GRO, GRF, D3, OUT,
    wsem, loc, d_s, d_r, g_s, g_r, w1_s, w1_r, w2_s, w2_r, w3_s, w3_r,
    r_s, r_r, gg_s, gg_r, l1_s, l1_r, l2_s, l2_r, t_s, t_r, q1_s, q1_r, q2_s, q2_r,
):
    t = lax.axis_index("tok")
    me = lax.axis_index("exp")
    core = lax.rem(t, 2)
    x = t // 2
    y = me // 8
    z = lax.rem(me, 8)
    xr, xl, xo = lax.rem(x + 1, 4), lax.rem(x + 3, 4), lax.rem(x + 2, 4)
    sib = t + 1 - 2 * core
    right, left, opp = 2 * xr + core, 2 * xl + core, 2 * xo + core
    a = jnp.where(core == 0, y, z)
    b = jnp.where(core == 0, z, y)
    sa = jnp.where(core == 0, 8, 1)
    sb = jnp.where(core == 0, 1, 8)

    barrier = pltpu.get_barrier_semaphore()

    first = [
        pltpu.make_async_copy(pl_h, PLV, loc.at[4]),
        pltpu.make_async_copy(tk_h, TK, loc.at[5]),
        pltpu.make_async_copy(og_h, OG, loc.at[6]),
        pltpu.make_async_copy(wr_h, WRL, loc.at[7]),
    ]
    for c in first:
        c.start()

    @pl.loop(1, NE)
    def _(k):
        pl.semaphore_signal(
            barrier, inc=1, device_id={"exp": lax.rem(me + k, NE)}, device_id_type=MESH
        )

    @pl.loop(1, NT)
    def _(k):
        pl.semaphore_signal(
            barrier, inc=1, device_id={"tok": lax.rem(t + k, NT)}, device_id_type=MESH
        )

    local = [
        pltpu.make_async_copy(wg_h, WG, wsem.at[0]),
        pltpu.make_async_copy(wu_h, WU, wsem.at[1]),
    ]
    for i in range(8):
        local.append(
            pltpu.make_async_copy(wd_h.at[:, pl.ds(512 * i, 512)], WD.at[i], wsem.at[2 + i])
        )
    for c in local:
        c.start()

    lane = lax.broadcasted_iota(jnp.int32, (128, 128), 1)
    expert = lax.broadcasted_iota(jnp.int32, (16, 64), 1)

    def pick_row(row):
        cols = []
        for n in range(8):
            line = jnp.where(expert == row * 8 + n, PLV[...].astype(F32), 0.0)
            cols.append(jnp.sum(line, axis=1, keepdims=True))
        pos = jnp.broadcast_to(jnp.concatenate(cols, axis=0).astype(jnp.int32), (128, 128))
        rows = pl.ds(pl.multiple_of(row * 128, 128), 128)
        for c in range(16):
            PT[rows, c * 128 : (c + 1) * 128] = jnp.where(pos == lane + 128 * c, 1.0, 0.0).astype(BF)
        oh = PT[rows, :]
        got = jnp.concatenate((dot(oh, TK[...], NTD), dot(oh, OG[...], NTD)), axis=1)
        S[pl.ds(row * 8, 8)] = got.astype(BF).reshape(8, 16, 128)

    for c in first:
        c.wait()
    WS[...] = jnp.where(core == 0, WRL[:, :128], WRL[:, 128:])

    def dispatch(i):
        sh = NEAR[i]
        row = lax.rem(y + sh, 8)
        pick_row(row)
        if i == 0:
            pl.semaphore_wait(barrier, NE - 1 + NT - 1)

        @pl.loop(1 if sh == 0 else 0, 8)
        def _(k):
            d = row * 8 + lax.rem(z + k, 8)
            remote(S.at[d], R.at[me], d_s, d_r.at[i], exp=d).start()

        if sh == 0:
            pltpu.make_async_copy(S.at[me], R.at[me], d_r.at[0]).start()

    for i in range(AHEAD):
        dispatch(i)

    own_half = pltpu.make_async_copy(WS, WM.at[a], loc.at[0])
    own_half.start()
    w1 = []
    for k in range(1, 8):
        w1.append(remote(WS, WM.at[a], w1_s, w1_r, exp=lax.rem(a + k, 8) * sa + b * sb))
        w1[-1].start()

    def router_second():
        own_half.wait()
        seven = WM.at[pl.ds(0, 7)]
        remote(seven, seven, w1_s, w1_r, exp=me).wait_recv()
        cs = []
        for k in range(1, 8):
            cs.append(
                remote(WM, WRF.at[core, b], w2_s, w2_r.at[k], exp=a * sa + lax.rem(b + k, 8) * sb)
            )
            cs[-1].start()
        c = pltpu.make_async_copy(WM, WRF.at[core, b], loc.at[1])
        c.start()
        c.wait()
        cs.append(remote(WRF.at[core, b], WRF.at[core, b], w3_s.at[0], w3_r.at[0], tok=sib))
        cs[-1].start()
        return cs

    def router_third(k):
        src = lax.rem(b + 8 - k, 8)
        remote(WM, WRF.at[core, src], w2_s, w2_r.at[k], exp=me).wait_recv()
        c = remote(WRF.at[core, src], WRF.at[core, src], w3_s.at[k], w3_r.at[k], tok=sib)
        c.start()
        return c

    low = lax.broadcasted_iota(jnp.int32, (16, 128), 1) < 64
    sent = []
    kept = {}

    def go(key, c):
        c.start()
        sent.append(c)
        kept[key] = c

    def gather_own(i):
        row = lax.rem(y + 8 - NEAR[i], 8)
        eight = R.at[pl.ds(row * 8, 8)]
        remote(eight, eight, d_s, d_r.at[i], exp=me).wait_recv()
        for m in range(4):
            p = R[row * 8 + 2 * m].astype(F32)
            q = R[row * 8 + 2 * m + 1].astype(F32)
            cols = slice(128 * m, 128 * m + 128)
            G2[row, t, 0, :, cols] = jnp.where(low, p, pltpu.roll(q, 64, 1)).astype(BF)
            G2[row, t, 1, :, cols] = jnp.where(low, pltpu.roll(p, 64, 1), q).astype(BF)
        blk = G2.at[row, t]
        go((0, i), remote(blk, blk, g_s.at[0, i], g_r.at[0, i], tok=right))
        go((1, i), remote(blk, blk, g_s.at[1, i], g_r.at[1, i], tok=left))
        go((2, i), remote(blk, blk, g_s.at[2, i], g_r.at[2, i], tok=sib))

    def gather_next(i):
        row = lax.rem(y + 8 - NEAR[i], 8)
        blk = G2.at[row, left]
        remote(blk, blk, g_s.at[0, i], g_r.at[0, i], tok=right).wait_recv()
        part = G2.at[row, left, 0]
        go((3, i), remote(part, part, g_s.at[3, i], g_r.at[3, i], tok=right))
        go((4, i), remote(blk, blk, g_s.at[4, i], g_r.at[4, i], tok=sib))
        blk = G2.at[row, right]
        remote(blk, blk, g_s.at[1, i], g_r.at[1, i], tok=left).wait_recv()
        part = G2.at[row, right, 1]
        go((5, i), remote(part, part, g_s.at[5, i], g_r.at[5, i], tok=left))
        go((6, i), remote(blk, blk, g_s.at[6, i], g_r.at[6, i], tok=sib))

    def gather_far(i):
        row = lax.rem(y + 8 - NEAR[i], 8)
        for h, kind in ((0, 3), (1, 5)):
            part = G2.at[row, opp, h]
            remote(part, part, g_s.at[kind, i], g_r.at[kind, i], tok=right).wait_recv()
            go((7 + h, i), remote(part, part, g_s.at[7 + h, i], g_r.at[7 + h, i], tok=sib))

    def gather_done(i):
        row = lax.rem(y + 8 - NEAR[i], 8)
        side = 1 - core
        for kind, who in ((2, sib), (4, 2 * xl + side), (6, 2 * xr + side)):
            blk = G2.at[row, who]
            remote(blk, blk, g_s.at[kind, i], g_r.at[kind, i], tok=sib).wait_recv()
        for h in (0, 1):
            part = G2.at[row, 2 * xo + side, h]
            remote(part, part, g_s.at[7 + h, i], g_r.at[7 + h, i], tok=sib).wait_recv()
        rows = G2[row, :, 0].reshape(128, 512)
        grads = G2[row, :, 1].reshape(128, 512)
        k = pl.ds(pl.multiple_of(row * 512, 512), 512)
        parts = (dot(rows, WG[k, :], NN), dot(rows, WU[k, :], NN), dot(grads, WD[row], NTD))
        for n, part in enumerate(parts):
            ACC[n] = part if i == 0 else ACC[n] + part

    w2 = None
    w3 = []
    for s in range(8 + LAG[2]):
        if s + AHEAD < 8:
            dispatch(s + AHEAD)
        if s < 8:
            gather_own(s)
        if s == 4:
            w2 = router_second()
        if 0 <= s - LAG[0] < 8:
            gather_next(s - LAG[0])
        if 0 <= s - LAG[1] < 8:
            gather_far(s - LAG[1])
        if s == LAG[2]:
            for c in local:
                c.wait()
        if 0 <= s - LAG[2] < 8:
            gather_done(s - LAG[2])
        if 1 <= s - RELAY < 8:
            w3.append(router_third(s - RELAY))

    pre_gate, pre_up, back = ACC[0], ACC[1], ACC[2]
    sg = jax.nn.sigmoid(pre_gate)
    hidden = (pre_gate * sg * pre_up).astype(BF)
    ACT[0] = hidden
    ACT[1] = (back * pre_up * sg * (1.0 + pre_gate * (1.0 - sg))).astype(BF)
    ACT[2] = (back * pre_gate * sg).astype(BF)
    gsum = jnp.sum(hidden.astype(F32) * back, axis=1, keepdims=True)
    GPB[...] = jnp.broadcast_to(gsum, (128, 128)).reshape(8, 16, 128)
    for k in range(1, 8):
        d = lax.rem(t + k, 8)
        remote(GPB.at[d], GPR.at[t], gg_s, gg_r, tok=d).start()
    pltpu.make_async_copy(GPB.at[t], GPR.at[t], gg_r).start()

    def sum_make(i):
        row = lax.rem(y + FAR[i], 8)
        k = pl.ds(pl.multiple_of(row * 512, 512), 512)
        eo = dot(ACT[0], WD[row], NN)
        PB[i, 0] = eo.astype(BF).reshape(4, 2, 16, 512)
        ri = dot(ACT[1], WG[k, :], NTD) + dot(ACT[2], WU[k, :], NTD)
        PB[i, 1] = ri.astype(BF).reshape(4, 2, 16, 512)
        go(("sib", i), remote(PB.at[i, :, :, 1 - core], SB.at[i], r_s.at[0, i], r_r.at[0, i], tok=sib))

    def sum_pair(i):
        kept["sib", i].wait_recv()
        PS[i] = (PB[i, :, :, core].astype(F32) + SB[i].astype(F32)).astype(BF)
        go(("le", i), remote(PS.at[i, 0, xo], B1.at[i, 0], r_s.at[1, i], r_r.at[1, i], tok=right))
        go(("lr", i), remote(PS.at[i, 1, xo], B1.at[i, 1], r_s.at[2, i], r_r.at[2, i], tok=left))
        go(("de", i), remote(PS.at[i, 0, xl], B3.at[i, 0], r_s.at[3, i], r_r.at[3, i], tok=left))
        go(("dr", i), remote(PS.at[i, 1, xr], B3.at[i, 1], r_s.at[4, i], r_r.at[4, i], tok=right))

    def sum_next(i):
        kept["le", i].wait_recv()
        C2[i, 0] = (PS[i, 0, xr].astype(F32) + B1[i, 0].astype(F32)).astype(BF)
        go(("ce", i), remote(C2.at[i, 0], B2.at[i, 0], r_s.at[5, i], r_r.at[5, i], tok=right))
        kept["lr", i].wait_recv()
        C2[i, 1] = (PS[i, 1, xl].astype(F32) + B1[i, 1].astype(F32)).astype(BF)
        go(("cr", i), remote(C2.at[i, 1], B2.at[i, 1], r_s.at[6, i], r_r.at[6, i], tok=left))

    def router():
        logits = [jnp.zeros((16, 128), F32), jnp.zeros((16, 128), F32)]
        for r in range(8):
            own = G2[r, t, 0]
            logits[0] += dot(own, WRF[0, :, r].reshape(512, 128), NN)
            logits[1] += dot(own, WRF[1, r].reshape(512, 128), NN)
        peak = jnp.maximum(
            jnp.max(logits[0], axis=1, keepdims=True), jnp.max(logits[1], axis=1, keepdims=True)
        )
        ex = [jnp.exp(v - peak) for v in logits]
        total = jnp.sum(ex[0], axis=1, keepdims=True) + jnp.sum(ex[1], axis=1, keepdims=True)
        probs = [v / total for v in ex]
        at = lax.broadcasted_iota(jnp.int32, (16, 128), 1)
        hit = [at == me * COLS, at + 128 == me * COLS]
        weight = sum(
            jnp.sum(jnp.where(m, v, 0.0), axis=1, keepdims=True) for m, v in zip(hit, probs)
        )
        eight = GPR.at[pl.ds(0, 8)]
        remote(eight, eight, gg_s, gg_r, tok=t).wait_recv()
        gate = GPR[0]
        for k in range(1, 8):
            gate = gate + GPR[k]
        scale = gate * weight
        for n in range(2):
            diff = jnp.where(hit[n], 1.0, 0.0) - probs[n]
            LQ[:, 128 * n : 128 * n + 128] = (diff * scale).astype(BF)
            for p in range(3):
                piece = diff.astype(BF)
                D3[n, 16 * p : 16 * p + 16] = piece
                diff = diff - piece.astype(F32)
        own_lq = pltpu.make_async_copy(LQ, LQM.at[a], loc.at[2])
        own_lq.start()
        for k in range(1, 8):
            remote(LQ, LQM.at[a], l1_s, l1_r, exp=lax.rem(a + k, 8) * sa + b * sb).start()
        return weight, scale, own_lq

    def router_grad_second(own_lq):
        own_lq.wait()
        seven = LQM.at[pl.ds(0, 7)]
        remote(seven, seven, l1_s, l1_r, exp=me).wait_recv()
        for k in range(1, 8):
            remote(LQM, LQR.at[b], l2_s, l2_r, exp=a * sa + lax.rem(b + k, 8) * sb).start()
        own = pltpu.make_async_copy(LQM, LQR.at[b], loc.at[3])
        own.start()
        return own

    def router_grad_sum(own):
        own.wait()
        seven = LQR.at[pl.ds(0, 7)]
        remote(seven, seven, l2_s, l2_r, exp=me).wait_recv()
        total = jnp.zeros((128, 256), F32)
        Sv = S[...].reshape(8, 8, 16, 128)
        for n in range(8):
            rows = jnp.where(core == 0, Sv[:, n].astype(F32), Sv[n].astype(F32)).astype(BF)
            total = total + dot(rows.reshape(128, 128), LQR[n].reshape(128, 256), TND)
        GRP[...] = total[:64].reshape(8, 8, 256)
        for k in range(1, 8):
            d = lax.rem(t + k, 8)
            remote(GRP.at[d], GRR.at[t], q1_s, q1_r, tok=d).start()
        pltpu.make_async_copy(GRP.at[t], GRR.at[t], q1_r).start()

    def router_grad_share():
        eight = GRR.at[pl.ds(0, 8)]
        remote(eight, eight, q1_s, q1_r, tok=t).wait_recv()
        total = GRR[0]
        for k in range(1, 8):
            total = total + GRR[k]
        GRO[...] = total
        for k in range(1, 8):
            remote(GRO, GRF.at[t], q2_s, q2_r, tok=lax.rem(t + k, 8)).start()
        pltpu.make_async_copy(GRO, GRF.at[t], q2_r).start()

    def finish(i, weight, scale):
        row = lax.rem(y + FAR[i], 8)
        for key in ("de", "dr", "ce", "cr"):
            kept[key, i].wait_recv()
        eo = PS[i, 0, x].astype(F32) + B2[i, 0].astype(F32) + B3[i, 0].astype(F32)
        ri = PS[i, 1, x].astype(F32) + B2[i, 1].astype(F32) + B3[i, 1].astype(F32)
        v3 = dot(D3[0], WRF[0, :, row].reshape(512, 128), NTD)
        v3 = v3 + dot(D3[1], WRF[1, row].reshape(512, 128), NTD)
        v = v3[0:16] + v3[16:32] + v3[32:48]
        for m in range(4):
            cols = slice(128 * m, 128 * m + 128)
            w = eo[:, cols] * weight
            g = ri[:, cols] * weight + v[:, cols] * scale
            TS[row * 8 + 2 * m] = jnp.where(low, w, pltpu.roll(g, 64, 1)).astype(BF)
            TS[row * 8 + 2 * m + 1] = jnp.where(low, pltpu.roll(w, 64, 1), g).astype(BF)

        @pl.loop(1 if FAR[i] == 0 else 0, 8)
        def _(k):
            d = row * 8 + lax.rem(z + k, 8)
            remote(TS.at[d], TR.at[me], t_s, t_r.at[i], exp=d).start()

        if FAR[i] == 0:
            pltpu.make_async_copy(TS.at[me], TR.at[me], t_r.at[i]).start()

    def router_ready():
        for k in range(8):
            src = lax.rem(jnp.where(core == 0, y, z) + 8 - k, 8)
            blk = WRF.at[1 - core, src]
            remote(blk, blk, w3_s.at[k], w3_r.at[k], tok=sib).wait_recv()

    def add_back(blocks, first, last):
        rows = []
        for i in blocks:
            rows.append(lax.rem(y + 8 - FAR[i], 8))
            eight = TR.at[pl.ds(rows[-1] * 8, 8)]
            remote(eight, eight, t_s, t_r.at[i], exp=me).wait_recv()
        tiles = [TR[pl.ds(r * 8, 8)].reshape(128, 128) for r in rows]
        for c in range(4):
            cols = slice(512 * c, 512 * c + 512)
            res = None if first else OUT[:, cols]
            for r, tile in zip(rows, tiles):
                hot = PT[pl.ds(pl.multiple_of(r * 128, 128), 128), cols]
                part = dot(tile, hot, TND)
                res = part if res is None else res + part
            if last:
                out_layer[:, cols] = res[:64].astype(BF)
                out_token[:, cols] = res[64:].astype(BF)
            else:
                OUT[:, cols] = res

    for s in range(8 + SLAG[2] + BACK):
        if s < 8:
            sum_make(s)
        if 0 <= s - SLAG[0] < 8:
            sum_pair(s - SLAG[0])
        if 0 <= s - SLAG[1] < 8:
            sum_next(s - SLAG[1])
        if s == ROUTE[0]:
            router_ready()
            weight, scale, own_lq = router()
        if s == ROUTE[1]:
            own = router_grad_second(own_lq)
        if s == ROUTE[2]:
            router_grad_sum(own)
        if s == ROUTE[3]:
            router_grad_share()
        if 0 <= s - SLAG[2] < 8:
            finish(s - SLAG[2], weight, scale)
        done = s - SLAG[2] - BACK
        if done == 3:
            add_back(range(0, 4), True, False)
        if done == 6:
            add_back(range(4, 7), False, False)
        if done == 7:
            add_back(range(7, 8), False, True)

    eight = GRF.at[pl.ds(0, 8)]
    remote(eight, eight, q2_s, q2_r, tok=t).wait_recv()
    out_router[...] = GRF[...].reshape(64, 256)

    for c in sent + w3 + w2[7:]:
        c.wait_send()
    n63 = S.at[pl.ds(0, 63)]
    remote(n63, n63, d_s, d_r.at[0], exp=me).wait_send()
    remote(n63, n63, t_s, t_r.at[0], exp=me).wait_send()
    n7 = WM.at[pl.ds(0, 7)]
    remote(n7, n7, w1_s, w1_r, exp=me).wait_send()
    n7 = WRF.at[0, pl.ds(0, 7)]
    remote(n7, n7, w2_s, w2_r.at[1], exp=me).wait_send()
    n7 = GPB.at[pl.ds(0, 7)]
    remote(n7, n7, gg_s, gg_r, tok=t).wait_send()
    n7 = LQM.at[pl.ds(0, 7)]
    remote(n7, n7, l1_s, l1_r, exp=me).wait_send()
    n7 = LQR.at[pl.ds(0, 7)]
    remote(n7, n7, l2_s, l2_r, exp=me).wait_send()
    n7 = GRP.at[pl.ds(0, 7)]
    remote(n7, n7, q1_s, q1_r, tok=t).wait_send()
    remote(n7, n7, q2_s, q2_r, tok=t).wait_send()


def body(tokens, w_router, pick_lists, w_gate, w_up, w_down, out_grad):
    V = pltpu.VMEM
    D = pltpu.SemaphoreType.DMA
    vm = pl.BlockSpec(memory_space=pltpu.VMEM)
    hbm = pl.BlockSpec(memory_space=pl.ANY)
    scratch = [
        V((64, 2048), BF),
        V((64, 2048), BF),
        V((64, 256), BF),
        V((16, 64), jnp.int32),
        V((1024, 2048), BF),
        V((64, 16, 128), BF),
        V((64, 16, 128), BF),
        V((8, 8, 2, 16, 512), BF),
        V((64, 128), BF),
        V((8, 64, 128), BF),
        V((2, 8, 8, 64, 128), BF),
        V((4096, 128), BF),
        V((4096, 128), BF),
        V((8, 128, 512), BF),
        V((3, 128, 128), F32),
        V((3, 128, 128), BF),
        V((8, 2, 4, 2, 16, 512), BF),
        V((8, 2, 4, 16, 512), BF),
        V((8, 2, 4, 16, 512), BF),
        V((8, 2, 16, 512), BF),
        V((8, 2, 16, 512), BF),
        V((8, 2, 16, 512), BF),
        V((8, 2, 16, 512), BF),
        V((8, 16, 128), F32),
        V((8, 16, 128), F32),
        V((16, 256), BF),
        V((8, 16, 256), BF),
        V((8, 8, 16, 256), BF),
        V((64, 16, 128), BF),
        V((64, 16, 128), BF),
        V((8, 8, 256), F32),
        V((8, 8, 256), F32),
        V((8, 256), F32),
        V((8, 8, 256), F32),
        V((2, 48, 128), BF),
        V((128, 2048), F32),
        D((10,)), D((8,)),
        D, D((8,)),
        D((9, 8)), D((9, 8)),
        D, D,
        D, D((8,)),
        D((8,)), D((8,)),
        D((7, 8)), D((7, 8)),
        D, D,
        D, D, D, D,
        D, D((8,)),
        D, D, D, D,
    ]
    shapes = (
        jax.ShapeDtypeStruct((64, 2048), BF),
        jax.ShapeDtypeStruct((64, 2048), BF),
        jax.ShapeDtypeStruct((64, 256), F32),
    )
    results = pl.pallas_call(
        kernel,
        out_shape=shapes,
        in_specs=[hbm] * 7,
        out_specs=(vm, vm, vm),
        scratch_shapes=scratch,
        compiler_params=pltpu.CompilerParams(
            collective_id=0, has_side_effects=True, vmem_limit_bytes=60 << 20
        ),
        cost_estimate=pl.CostEstimate(
            flops=3_000_000_000, bytes_accessed=8_000_000, transcendentals=40_000
        ),
        name="experts",
    )(tokens, out_grad, w_router, pick_lists[0].T, w_gate[0], w_up[0], w_down[0])
    return pl.pallas_call(
        hand_over,
        out_shape=shapes,
        in_specs=[vm] * 3,
        out_specs=(hbm,) * 3,
        scratch_shapes=[D((3,))],
        name="results",
    )(*results)


def hand_over(a, b, c, ra, rb, rc, sem):
    copies = [
        pltpu.make_async_copy(src, dst, sem.at[n])
        for n, (src, dst) in enumerate(((a, ra), (b, rb), (c, rc)))
    ]
    for copy in copies:
        copy.start()
    for copy in copies:
        copy.wait()


def solution(mesh):
    placed = (
        P("exp", "tok"),
        P("exp", None),
        P("tok", None, None),
        P("exp", None, "tok"),
        P("exp", None, "tok"),
        P("exp", "tok", None),
        P("exp", "tok"),
    )
    return jax.shard_map(
        body,
        mesh=mesh,
        in_specs=placed,
        out_specs=(P("exp", "tok"), P("exp", "tok"), P("exp", None)),
        check_vma=False,
    )
```

```python
import jax
import jax.numpy as jnp
from jax import lax
from jax.experimental import pallas as pl
from jax.experimental.pallas import tpu as pltpu
from jax.sharding import PartitionSpec as P

MESH = pl.DeviceIdType.MESH
BF = jnp.bfloat16
F32 = jnp.float32
NE = 64
NT = 8
CAP = 16
COLS = 4
NEAR = (0, 1, 7, 2, 6, 3, 5, 4)
FAR = (4, 3, 5, 2, 6, 1, 7, 0)
AHEAD = 8
LAG = (3, 6, 8)
SLAG = (2, 4, 6)
RELAY = 8
ROUTE = (2, 5, 9, 12)
BACK = 3
NN = (((1,), (0,)), ((), ()))
NTD = (((1,), (1,)), ((), ()))
TND = (((0,), (0,)), ((), ()))


def dot(a, b, dims):
    return lax.dot_general(a, b, dims, preferred_element_type=F32)


def remote(src, dst, send, recv, **where):
    return pltpu.make_async_remote_copy(
        src, dst, send, recv, device_id=where, device_id_type=MESH
    )


def kernel(
    tk_h, og_h, wr_h, pl_h, wg_h, wu_h, wd_h,
    out_layer, out_token, out_router,
    TK, OG, WRL, PLV, PT, S, R, G2, WS, WM, WRF, WG, WU, WD, ACC, ACT,
    PB, SB, PS, B1, B2, B3, C2, GPB, GPR, LQ, LQM, LQR, TS, TR, GRP, GRR, GRO, GRF, D3, OUT,
    wsem, loc, d_s, d_r, g_s, g_r, w1_s, w1_r, w2_s, w2_r, w3_s, w3_r,
    r_s, r_r, gg_s, gg_r, l1_s, l1_r, l2_s, l2_r, t_s, t_r, q1_s, q1_r, q2_s, q2_r,
):
    t = lax.axis_index("tok")
    me = lax.axis_index("exp")
    core = lax.rem(t, 2)
    x = t // 2
    y = me // 8
    z = lax.rem(me, 8)
    xr, xl, xo = lax.rem(x + 1, 4), lax.rem(x + 3, 4), lax.rem(x + 2, 4)
    sib = t + 1 - 2 * core
    right, left, opp = 2 * xr + core, 2 * xl + core, 2 * xo + core
    a = jnp.where(core == 0, y, z)
    b = jnp.where(core == 0, z, y)
    sa = jnp.where(core == 0, 8, 1)
    sb = jnp.where(core == 0, 1, 8)

    barrier = pltpu.get_barrier_semaphore()

    first = [
        pltpu.make_async_copy(pl_h, PLV, loc.at[4]),
        pltpu.make_async_copy(tk_h, TK, loc.at[5]),
        pltpu.make_async_copy(og_h, OG, loc.at[6]),
        pltpu.make_async_copy(wr_h, WRL, loc.at[7]),
    ]
    for c in first:
        c.start()

    for k in range(1, NE):
        pl.semaphore_signal(
            barrier, inc=1, device_id={"exp": lax.rem(me + k, NE)}, device_id_type=MESH
        )

    for k in range(1, NT):
        pl.semaphore_signal(
            barrier, inc=1, device_id={"tok": lax.rem(t + k, NT)}, device_id_type=MESH
        )

    local = [
        pltpu.make_async_copy(wg_h, WG, wsem.at[0]),
        pltpu.make_async_copy(wu_h, WU, wsem.at[1]),
    ]
    for i in range(8):
        local.append(
            pltpu.make_async_copy(wd_h.at[:, pl.ds(512 * i, 512)], WD.at[i], wsem.at[2 + i])
        )
    for c in local:
        c.start()

    lane = lax.broadcasted_iota(jnp.int32, (128, 128), 1)
    expert = lax.broadcasted_iota(jnp.int32, (16, 64), 1)

    def pick_row(row):
        cols = []
        for n in range(8):
            line = jnp.where(expert == row * 8 + n, PLV[...].astype(F32), 0.0)
            cols.append(jnp.sum(line, axis=1, keepdims=True))
        pos = jnp.broadcast_to(jnp.concatenate(cols, axis=0).astype(jnp.int32), (128, 128))
        rows = pl.ds(pl.multiple_of(row * 128, 128), 128)
        for c in range(16):
            PT[rows, c * 128 : (c + 1) * 128] = jnp.where(pos == lane + 128 * c, 1.0, 0.0).astype(BF)
        oh = PT[rows, :]
        got = jnp.concatenate((dot(oh, TK[...], NTD), dot(oh, OG[...], NTD)), axis=1)
        S[pl.ds(row * 8, 8)] = got.astype(BF).reshape(8, 16, 128)

    for c in first:
        c.wait()
    WS[...] = jnp.where(core == 0, WRL[:, :128], WRL[:, 128:])

    def dispatch(i):
        sh = NEAR[i]
        row = lax.rem(y + sh, 8)
        pick_row(row)
        if i == 0:
            pl.semaphore_wait(barrier, NE - 1 + NT - 1)

        @pl.loop(1 if sh == 0 else 0, 8)
        def _(k):
            d = row * 8 + lax.rem(z + k, 8)
            remote(S.at[d], R.at[me], d_s, d_r.at[i], exp=d).start()

        if sh == 0:
            pltpu.make_async_copy(S.at[me], R.at[me], d_r.at[0]).start()

    for i in range(AHEAD):
        dispatch(i)

    own_half = pltpu.make_async_copy(WS, WM.at[a], loc.at[0])
    own_half.start()
    w1 = []
    for k in range(1, 8):
        w1.append(remote(WS, WM.at[a], w1_s, w1_r, exp=lax.rem(a + k, 8) * sa + b * sb))
        w1[-1].start()

    def router_second():
        own_half.wait()
        seven = WM.at[pl.ds(0, 7)]
        remote(seven, seven, w1_s, w1_r, exp=me).wait_recv()
        cs = []
        for k in range(1, 8):
            cs.append(
                remote(WM, WRF.at[core, b], w2_s, w2_r.at[k], exp=a * sa + lax.rem(b + k, 8) * sb)
            )
            cs[-1].start()
        c = pltpu.make_async_copy(WM, WRF.at[core, b], loc.at[1])
        c.start()
        c.wait()
        cs.append(remote(WRF.at[core, b], WRF.at[core, b], w3_s.at[0], w3_r.at[0], tok=sib))
        cs[-1].start()
        return cs

    def router_third(k):
        src = lax.rem(b + 8 - k, 8)
        remote(WM, WRF.at[core, src], w2_s, w2_r.at[k], exp=me).wait_recv()
        c = remote(WRF.at[core, src], WRF.at[core, src], w3_s.at[k], w3_r.at[k], tok=sib)
        c.start()
        return c

    low = lax.broadcasted_iota(jnp.int32, (16, 128), 1) < 64
    sent = []
    kept = {}

    def go(key, c):
        c.start()
        sent.append(c)
        kept[key] = c

    def gather_own(i):
        row = lax.rem(y + 8 - NEAR[i], 8)
        eight = R.at[pl.ds(row * 8, 8)]
        remote(eight, eight, d_s, d_r.at[i], exp=me).wait_recv()
        for m in range(4):
            p = R[row * 8 + 2 * m].astype(F32)
            q = R[row * 8 + 2 * m + 1].astype(F32)
            cols = slice(128 * m, 128 * m + 128)
            G2[row, t, 0, :, cols] = jnp.where(low, p, pltpu.roll(q, 64, 1)).astype(BF)
            G2[row, t, 1, :, cols] = jnp.where(low, pltpu.roll(p, 64, 1), q).astype(BF)
        blk = G2.at[row, t]
        go((0, i), remote(blk, blk, g_s.at[0, i], g_r.at[0, i], tok=right))
        go((1, i), remote(blk, blk, g_s.at[1, i], g_r.at[1, i], tok=left))
        go((2, i), remote(blk, blk, g_s.at[2, i], g_r.at[2, i], tok=sib))

    def gather_next(i):
        row = lax.rem(y + 8 - NEAR[i], 8)
        blk = G2.at[row, left]
        remote(blk, blk, g_s.at[0, i], g_r.at[0, i], tok=right).wait_recv()
        part = G2.at[row, left, 0]
        go((3, i), remote(part, part, g_s.at[3, i], g_r.at[3, i], tok=right))
        go((4, i), remote(blk, blk, g_s.at[4, i], g_r.at[4, i], tok=sib))
        blk = G2.at[row, right]
        remote(blk, blk, g_s.at[1, i], g_r.at[1, i], tok=left).wait_recv()
        part = G2.at[row, right, 1]
        go((5, i), remote(part, part, g_s.at[5, i], g_r.at[5, i], tok=left))
        go((6, i), remote(blk, blk, g_s.at[6, i], g_r.at[6, i], tok=sib))

    def gather_far(i):
        row = lax.rem(y + 8 - NEAR[i], 8)
        for h, kind in ((0, 3), (1, 5)):
            part = G2.at[row, opp, h]
            remote(part, part, g_s.at[kind, i], g_r.at[kind, i], tok=right).wait_recv()
            go((7 + h, i), remote(part, part, g_s.at[7 + h, i], g_r.at[7 + h, i], tok=sib))

    def gather_done(i):
        row = lax.rem(y + 8 - NEAR[i], 8)
        side = 1 - core
        for kind, who in ((2, sib), (4, 2 * xl + side), (6, 2 * xr + side)):
            blk = G2.at[row, who]
            remote(blk, blk, g_s.at[kind, i], g_r.at[kind, i], tok=sib).wait_recv()
        for h in (0, 1):
            part = G2.at[row, 2 * xo + side, h]
            remote(part, part, g_s.at[7 + h, i], g_r.at[7 + h, i], tok=sib).wait_recv()
        rows = G2[row, :, 0].reshape(128, 512)
        grads = G2[row, :, 1].reshape(128, 512)
        k = pl.ds(pl.multiple_of(row * 512, 512), 512)
        parts = (dot(rows, WG[k, :], NN), dot(rows, WU[k, :], NN), dot(grads, WD[row], NTD))
        for n, part in enumerate(parts):
            ACC[n] = part if i == 0 else ACC[n] + part

    w2 = None
    w3 = []
    for s in range(8 + LAG[2]):
        if s + AHEAD < 8:
            dispatch(s + AHEAD)
        if s < 8:
            gather_own(s)
        if s == 4:
            w2 = router_second()
        if 0 <= s - LAG[0] < 8:
            gather_next(s - LAG[0])
        if 0 <= s - LAG[1] < 8:
            gather_far(s - LAG[1])
        if s == LAG[2]:
            for c in local:
                c.wait()
        if 0 <= s - LAG[2] < 8:
            gather_done(s - LAG[2])
        if 1 <= s - RELAY < 8:
            w3.append(router_third(s - RELAY))

    pre_gate, pre_up, back = ACC[0], ACC[1], ACC[2]
    sg = jax.nn.sigmoid(pre_gate)
    hidden = (pre_gate * sg * pre_up).astype(BF)
    ACT[0] = hidden
    ACT[1] = (back * pre_up * sg * (1.0 + pre_gate * (1.0 - sg))).astype(BF)
    ACT[2] = (back * pre_gate * sg).astype(BF)
    gsum = jnp.sum(hidden.astype(F32) * back, axis=1, keepdims=True)
    GPB[...] = jnp.broadcast_to(gsum, (128, 128)).reshape(8, 16, 128)
    for k in range(1, 8):
        d = lax.rem(t + k, 8)
        remote(GPB.at[d], GPR.at[t], gg_s, gg_r, tok=d).start()
    pltpu.make_async_copy(GPB.at[t], GPR.at[t], gg_r).start()

    def sum_make(i):
        row = lax.rem(y + FAR[i], 8)
        k = pl.ds(pl.multiple_of(row * 512, 512), 512)
        eo = dot(ACT[0], WD[row], NN)
        PB[i, 0] = eo.astype(BF).reshape(4, 2, 16, 512)
        ri = dot(ACT[1], WG[k, :], NTD) + dot(ACT[2], WU[k, :], NTD)
        PB[i, 1] = ri.astype(BF).reshape(4, 2, 16, 512)
        go(("sib", i), remote(PB.at[i, :, :, 1 - core], SB.at[i], r_s.at[0, i], r_r.at[0, i], tok=sib))

    def sum_pair(i):
        kept["sib", i].wait_recv()
        PS[i] = (PB[i, :, :, core].astype(F32) + SB[i].astype(F32)).astype(BF)
        go(("le", i), remote(PS.at[i, 0, xo], B1.at[i, 0], r_s.at[1, i], r_r.at[1, i], tok=right))
        go(("lr", i), remote(PS.at[i, 1, xo], B1.at[i, 1], r_s.at[2, i], r_r.at[2, i], tok=left))
        go(("de", i), remote(PS.at[i, 0, xl], B3.at[i, 0], r_s.at[3, i], r_r.at[3, i], tok=left))
        go(("dr", i), remote(PS.at[i, 1, xr], B3.at[i, 1], r_s.at[4, i], r_r.at[4, i], tok=right))

    def sum_next(i):
        kept["le", i].wait_recv()
        C2[i, 0] = (PS[i, 0, xr].astype(F32) + B1[i, 0].astype(F32)).astype(BF)
        go(("ce", i), remote(C2.at[i, 0], B2.at[i, 0], r_s.at[5, i], r_r.at[5, i], tok=right))
        kept["lr", i].wait_recv()
        C2[i, 1] = (PS[i, 1, xl].astype(F32) + B1[i, 1].astype(F32)).astype(BF)
        go(("cr", i), remote(C2.at[i, 1], B2.at[i, 1], r_s.at[6, i], r_r.at[6, i], tok=left))

    def router():
        logits = [jnp.zeros((16, 128), F32), jnp.zeros((16, 128), F32)]
        for r in range(8):
            own = G2[r, t, 0]
            logits[0] += dot(own, WRF[0, :, r].reshape(512, 128), NN)
            logits[1] += dot(own, WRF[1, r].reshape(512, 128), NN)
        peak = jnp.maximum(
            jnp.max(logits[0], axis=1, keepdims=True), jnp.max(logits[1], axis=1, keepdims=True)
        )
        ex = [jnp.exp(v - peak) for v in logits]
        total = jnp.sum(ex[0], axis=1, keepdims=True) + jnp.sum(ex[1], axis=1, keepdims=True)
        probs = [v / total for v in ex]
        at = lax.broadcasted_iota(jnp.int32, (16, 128), 1)
        hit = [at == me * COLS, at + 128 == me * COLS]
        weight = sum(
            jnp.sum(jnp.where(m, v, 0.0), axis=1, keepdims=True) for m, v in zip(hit, probs)
        )
        eight = GPR.at[pl.ds(0, 8)]
        remote(eight, eight, gg_s, gg_r, tok=t).wait_recv()
        gate = GPR[0]
        for k in range(1, 8):
            gate = gate + GPR[k]
        scale = gate * weight
        for n in range(2):
            diff = jnp.where(hit[n], 1.0, 0.0) - probs[n]
            LQ[:, 128 * n : 128 * n + 128] = (diff * scale).astype(BF)
            for p in range(3):
                piece = diff.astype(BF)
                D3[n, 16 * p : 16 * p + 16] = piece
                diff = diff - piece.astype(F32)
        own_lq = pltpu.make_async_copy(LQ, LQM.at[a], loc.at[2])
        own_lq.start()
        for k in range(1, 8):
            remote(LQ, LQM.at[a], l1_s, l1_r, exp=lax.rem(a + k, 8) * sa + b * sb).start()
        return weight, scale, own_lq

    def router_grad_second(own_lq):
        own_lq.wait()
        seven = LQM.at[pl.ds(0, 7)]
        remote(seven, seven, l1_s, l1_r, exp=me).wait_recv()
        for k in range(1, 8):
            remote(LQM, LQR.at[b], l2_s, l2_r, exp=a * sa + lax.rem(b + k, 8) * sb).start()
        own = pltpu.make_async_copy(LQM, LQR.at[b], loc.at[3])
        own.start()
        return own

    def router_grad_sum(own):
        own.wait()
        seven = LQR.at[pl.ds(0, 7)]
        remote(seven, seven, l2_s, l2_r, exp=me).wait_recv()
        total = jnp.zeros((128, 256), F32)
        Sv = S[...].reshape(8, 8, 16, 128)
        for n in range(8):
            rows = jnp.where(core == 0, Sv[:, n].astype(F32), Sv[n].astype(F32)).astype(BF)
            total = total + dot(rows.reshape(128, 128), LQR[n].reshape(128, 256), TND)
        GRP[...] = total[:64].reshape(8, 8, 256)
        for k in range(1, 8):
            d = lax.rem(t + k, 8)
            remote(GRP.at[d], GRR.at[t], q1_s, q1_r, tok=d).start()
        pltpu.make_async_copy(GRP.at[t], GRR.at[t], q1_r).start()

    def router_grad_share():
        eight = GRR.at[pl.ds(0, 8)]
        remote(eight, eight, q1_s, q1_r, tok=t).wait_recv()
        total = GRR[0]
        for k in range(1, 8):
            total = total + GRR[k]
        GRO[...] = total
        for k in range(1, 8):
            remote(GRO, GRF.at[t], q2_s, q2_r, tok=lax.rem(t + k, 8)).start()
        pltpu.make_async_copy(GRO, GRF.at[t], q2_r).start()

    def finish(i, weight, scale):
        row = lax.rem(y + FAR[i], 8)
        for key in ("de", "dr", "ce", "cr"):
            kept[key, i].wait_recv()
        eo = PS[i, 0, x].astype(F32) + B2[i, 0].astype(F32) + B3[i, 0].astype(F32)
        ri = PS[i, 1, x].astype(F32) + B2[i, 1].astype(F32) + B3[i, 1].astype(F32)
        v3 = dot(D3[0], WRF[0, :, row].reshape(512, 128), NTD)
        v3 = v3 + dot(D3[1], WRF[1, row].reshape(512, 128), NTD)
        v = v3[0:16] + v3[16:32] + v3[32:48]
        for m in range(4):
            cols = slice(128 * m, 128 * m + 128)
            w = eo[:, cols] * weight
            g = ri[:, cols] * weight + v[:, cols] * scale
            TS[row * 8 + 2 * m] = jnp.where(low, w, pltpu.roll(g, 64, 1)).astype(BF)
            TS[row * 8 + 2 * m + 1] = jnp.where(low, pltpu.roll(w, 64, 1), g).astype(BF)

        @pl.loop(1 if FAR[i] == 0 else 0, 8)
        def _(k):
            d = row * 8 + lax.rem(z + k, 8)
            remote(TS.at[d], TR.at[me], t_s, t_r.at[i], exp=d).start()

        if FAR[i] == 0:
            pltpu.make_async_copy(TS.at[me], TR.at[me], t_r.at[i]).start()

    def router_ready():
        for k in range(8):
            src = lax.rem(jnp.where(core == 0, y, z) + 8 - k, 8)
            blk = WRF.at[1 - core, src]
            remote(blk, blk, w3_s.at[k], w3_r.at[k], tok=sib).wait_recv()

    def add_back(blocks, first, last):
        rows = []
        for i in blocks:
            rows.append(lax.rem(y + 8 - FAR[i], 8))
            eight = TR.at[pl.ds(rows[-1] * 8, 8)]
            remote(eight, eight, t_s, t_r.at[i], exp=me).wait_recv()
        tiles = [TR[pl.ds(r * 8, 8)].reshape(128, 128) for r in rows]
        for c in range(4):
            cols = slice(512 * c, 512 * c + 512)
            res = None if first else OUT[:, cols]
            for r, tile in zip(rows, tiles):
                hot = PT[pl.ds(pl.multiple_of(r * 128, 128), 128), cols]
                part = dot(tile, hot, TND)
                res = part if res is None else res + part
            if last:
                out_layer[:, cols] = res[:64].astype(BF)
                out_token[:, cols] = res[64:].astype(BF)
            else:
                OUT[:, cols] = res

    for s in range(8 + SLAG[2] + BACK):
        if s < 8:
            sum_make(s)
        if 0 <= s - SLAG[0] < 8:
            sum_pair(s - SLAG[0])
        if 0 <= s - SLAG[1] < 8:
            sum_next(s - SLAG[1])
        if s == ROUTE[0]:
            router_ready()
            weight, scale, own_lq = router()
        if s == ROUTE[1]:
            own = router_grad_second(own_lq)
        if s == ROUTE[2]:
            router_grad_sum(own)
        if s == ROUTE[3]:
            router_grad_share()
        if 0 <= s - SLAG[2] < 8:
            finish(s - SLAG[2], weight, scale)
        done = s - SLAG[2] - BACK
        if done == 3:
            add_back(range(0, 4), True, False)
        if done == 6:
            add_back(range(4, 7), False, False)
        if done == 7:
            add_back(range(7, 8), False, True)

    eight = GRF.at[pl.ds(0, 8)]
    remote(eight, eight, q2_s, q2_r, tok=t).wait_recv()
    out_router[...] = GRF[...].reshape(64, 256)

    for c in sent + w3 + w2[7:]:
        c.wait_send()
    n63 = S.at[pl.ds(0, 63)]
    remote(n63, n63, d_s, d_r.at[0], exp=me).wait_send()
    remote(n63, n63, t_s, t_r.at[0], exp=me).wait_send()
    n7 = WM.at[pl.ds(0, 7)]
    remote(n7, n7, w1_s, w1_r, exp=me).wait_send()
    n7 = WRF.at[0, pl.ds(0, 7)]
    remote(n7, n7, w2_s, w2_r.at[1], exp=me).wait_send()
    n7 = GPB.at[pl.ds(0, 7)]
    remote(n7, n7, gg_s, gg_r, tok=t).wait_send()
    n7 = LQM.at[pl.ds(0, 7)]
    remote(n7, n7, l1_s, l1_r, exp=me).wait_send()
    n7 = LQR.at[pl.ds(0, 7)]
    remote(n7, n7, l2_s, l2_r, exp=me).wait_send()
    n7 = GRP.at[pl.ds(0, 7)]
    remote(n7, n7, q1_s, q1_r, tok=t).wait_send()
    remote(n7, n7, q2_s, q2_r, tok=t).wait_send()


def body(tokens, w_router, pick_lists, w_gate, w_up, w_down, out_grad):
    V = pltpu.VMEM
    D = pltpu.SemaphoreType.DMA
    vm = pl.BlockSpec(memory_space=pltpu.VMEM)
    hbm = pl.BlockSpec(memory_space=pl.ANY)
    scratch = [
        V((64, 2048), BF),
        V((64, 2048), BF),
        V((64, 256), BF),
        V((16, 64), jnp.int32),
        V((1024, 2048), BF),
        V((64, 16, 128), BF),
        V((64, 16, 128), BF),
        V((8, 8, 2, 16, 512), BF),
        V((64, 128), BF),
        V((8, 64, 128), BF),
        V((2, 8, 8, 64, 128), BF),
        V((4096, 128), BF),
        V((4096, 128), BF),
        V((8, 128, 512), BF),
        V((3, 128, 128), F32),
        V((3, 128, 128), BF),
        V((8, 2, 4, 2, 16, 512), BF),
        V((8, 2, 4, 16, 512), BF),
        V((8, 2, 4, 16, 512), BF),
        V((8, 2, 16, 512), BF),
        V((8, 2, 16, 512), BF),
        V((8, 2, 16, 512), BF),
        V((8, 2, 16, 512), BF),
        V((8, 16, 128), F32),
        V((8, 16, 128), F32),
        V((16, 256), BF),
        V((8, 16, 256), BF),
        V((8, 8, 16, 256), BF),
        V((64, 16, 128), BF),
        V((64, 16, 128), BF),
        V((8, 8, 256), F32),
        V((8, 8, 256), F32),
        V((8, 256), F32),
        V((8, 8, 256), F32),
        V((2, 48, 128), BF),
        V((128, 2048), F32),
        D((10,)), D((8,)),
        D, D((8,)),
        D((9, 8)), D((9, 8)),
        D, D,
        D, D((8,)),
        D((8,)), D((8,)),
        D((7, 8)), D((7, 8)),
        D, D,
        D, D, D, D,
        D, D((8,)),
        D, D, D, D,
    ]
    shapes = (
        jax.ShapeDtypeStruct((64, 2048), BF),
        jax.ShapeDtypeStruct((64, 2048), BF),
        jax.ShapeDtypeStruct((64, 256), F32),
    )
    results = pl.pallas_call(
        kernel,
        out_shape=shapes,
        in_specs=[hbm] * 7,
        out_specs=(vm, vm, vm),
        scratch_shapes=scratch,
        compiler_params=pltpu.CompilerParams(
            collective_id=0, has_side_effects=True, vmem_limit_bytes=60 << 20
        ),
        cost_estimate=pl.CostEstimate(
            flops=3_000_000_000, bytes_accessed=8_000_000, transcendentals=40_000
        ),
        name="experts",
    )(tokens, out_grad, w_router, pick_lists[0].T, w_gate[0], w_up[0], w_down[0])
    return pl.pallas_call(
        hand_over,
        out_shape=shapes,
        in_specs=[vm] * 3,
        out_specs=(hbm,) * 3,
        scratch_shapes=[D((3,))],
        name="results",
    )(*results)


def hand_over(a, b, c, ra, rb, rc, sem):
    copies = [
        pltpu.make_async_copy(src, dst, sem.at[n])
        for n, (src, dst) in enumerate(((a, ra), (b, rb), (c, rc)))
    ]
    for copy in copies:
        copy.start()
    for copy in copies:
        copy.wait()


def solution(mesh):
    placed = (
        P("exp", "tok"),
        P("exp", None),
        P("tok", None, None),
        P("exp", None, "tok"),
        P("exp", None, "tok"),
        P("exp", "tok", None),
        P("exp", "tok"),
    )
    return jax.shard_map(
        body,
        mesh=mesh,
        in_specs=placed,
        out_specs=(P("exp", "tok"), P("exp", "tok"), P("exp", None)),
        check_vma=False,
    )
```
